32 devices in a mesh: groups: 2 (over x), row: 16 (over z, y, core).
Axes of the slice: x: 2, y: 2, z: 4, core: 2. Of those that a mesh axis runs over, the one named last changes fastest.
Arguments:
- tokens: bfloat16 [32, 64, 1024], P(('groups', 'row')), parts along dimension 0, may hold values from -6 to 6
- gate_weight: bfloat16 [16, 1024, 2048], P('row'), may hold values from -0.09375 to 0.09375
- up_weight: bfloat16 [16, 1024, 2048], P('row'), may hold values from -0.09375 to 0.09375
- down_weight: bfloat16 [16, 2048, 1024], P('row'), may hold values from -0.0625 to 0.0625
- cotangent: bfloat16 [32, 64, 1024], P(('groups', 'row')), parts along dimension 0, may hold values from -6 to 6
Outputs:
- mixed: bfloat16 [32, 64, 1024], P(('groups', 'row')), parts along dimension 0
- input_grad: bfloat16 [32, 64, 1024], P(('groups', 'row')), parts along dimension 0
- gate_grad: float32 [32, 1024, 2048], P(('groups', 'row')), parts along dimension 0
- up_grad: float32 [32, 1024, 2048], P(('groups', 'row')), parts along dimension 0
- down_grad: float32 [32, 2048, 1024], P(('groups', 'row')), parts along dimension 0
The draws below stay inside these ranges and needn't reach their ends.
There are 2 independent parts, one for each index of `groups`. The reference program is written for one: setup_inputs(seed, part) draws one part's arguments, and reference() takes and returns one part's arrays. A program takes and returns all parts, laid end to end along the dimension named above; an argument that names none is the same for every part. Nothing has to cross between parts.
All inputs are finite; a program needn't handle non-finite values.
Results may differ from the reference program's by a relative error of at most 0.005.
Values may be sent and summed in bfloat16 or wider, within the bound.
No kernel may reach another device: no remote copies, remote signals or barrier semaphores. Data moves between devices by JAX's collectives and lax.ppermute only.
A program may use at most 128 MiB of HBM per device.

```python
import jax
import jax.numpy as jnp

D = 4096
FF = 8192
TOK_ROW = 64
GRID = 4
TOKENS = 256
N_ROW = 16


def steps_of(own_key, shape, split, low, top_value):
    def one(position, shards_of):
        steps = jax.random.uniform(jax.random.fold_in(jax.random.fold_in(own_key, 6), position), (shards_of,), jnp.float32, low / len(split), top_value / len(split))
        return jnp.repeat(jnp.exp(steps), shape[position] // shards_of).reshape((-1,) + (1,) * (len(shape) - position - 1))

    gain = one(*split[0])
    for cut in split[1:]:
        gain = gain * one(*cut)
    return gain


def normal_values(rng, dims, scale, bound, cuts=(), dtype=jnp.bfloat16):
    values = jax.random.normal(rng, dims, jnp.float32) * scale
    if len(cuts) > 0:
        values = steps_of(rng, dims, cuts, -0.22, 0.18) * values
    return jnp.clip(values, min=-bound, max=bound).astype(dtype)


def setup_inputs(seed: int = 0, part: int = 0) -> dict:
    key_list = jax.random.split(jax.random.key(seed), 6)
    own_keys = jax.random.split(jax.random.fold_in(key_list[5], part), 6)
    return {
        "tokens": normal_values(own_keys[0], (N_ROW, TOK_ROW, D // GRID), 1.0, 6.0, ((0, 16),)),
        "gate_weight": normal_values(key_list[1], (N_ROW, D // GRID, FF // GRID), D ** -0.5, 0.09375, ((0, 16),)),
        "up_weight": normal_values(key_list[2], (N_ROW, D // GRID, FF // GRID), D ** -0.5, 0.09375, ((0, 16),)),
        "down_weight": normal_values(key_list[3], (N_ROW, FF // GRID, D // GRID), FF ** -0.5, 0.0625, ((0, 16),)),
        "cotangent": normal_values(own_keys[4], (N_ROW, TOK_ROW, D // GRID), 1.0, 6.0, ((0, 16),)),
    }


def token_matrix(blocks):
    return blocks.reshape(GRID, GRID, TOK_ROW, D // GRID).transpose(1, 2, 0, 3).reshape(TOKENS, D)


def token_blocks(full):
    return full.reshape(GRID, TOK_ROW, GRID, D // GRID).transpose(2, 0, 1, 3).reshape(N_ROW, TOK_ROW, D // GRID)


def weight_matrix(blocks):
    return blocks.reshape(GRID, GRID, D // GRID, FF // GRID).transpose(0, 2, 1, 3).reshape(D, FF)


def weight_blocks(full):
    return full.reshape(GRID, D // GRID, GRID, FF // GRID).transpose(0, 2, 1, 3).reshape(N_ROW, D // GRID, FF // GRID)


def down_matrix(blocks):
    return blocks.reshape(GRID, GRID, FF // GRID, D // GRID).transpose(1, 2, 0, 3).reshape(FF, D)


def down_blocks(full):
    return full.reshape(GRID, FF // GRID, GRID, D // GRID).transpose(2, 0, 1, 3).reshape(N_ROW, FF // GRID, D // GRID)


def reference(tokens, gate_weight, up_weight, down_weight, cotangent):
    inputs = token_matrix(tokens)
    outgrad = token_matrix(cotangent)
    w_gate = weight_matrix(gate_weight)
    w_up = weight_matrix(up_weight)
    w_down = down_matrix(down_weight)
    gate = jnp.dot(inputs, w_gate, preferred_element_type=jnp.float32)
    up = jnp.dot(inputs, w_up, preferred_element_type=jnp.float32)
    sigma = jax.nn.sigmoid(gate)
    activated = gate * sigma
    hidden = (activated * up).astype(jnp.bfloat16)
    layer_out = jnp.dot(hidden, w_down, preferred_element_type=jnp.float32).astype(jnp.bfloat16)
    hidden_grad = jnp.dot(outgrad, w_down.T, preferred_element_type=jnp.float32)
    gate_delta = (hidden_grad * up * sigma * (1.0 + gate * (1.0 - sigma))).astype(jnp.bfloat16)
    up_delta = (hidden_grad * activated).astype(jnp.bfloat16)
    down_grad = jnp.dot(hidden.T, outgrad, preferred_element_type=jnp.float32)
    gate_grad = jnp.dot(inputs.T, gate_delta, preferred_element_type=jnp.float32)
    up_grad = jnp.dot(inputs.T, up_delta, preferred_element_type=jnp.float32)
    input_full = (jnp.dot(gate_delta, w_gate.T, preferred_element_type=jnp.float32)
                  + jnp.dot(up_delta, w_up.T, preferred_element_type=jnp.float32)).astype(jnp.bfloat16)
    return (token_blocks(layer_out), token_blocks(input_full), weight_blocks(gate_grad),
            weight_blocks(up_grad), down_blocks(down_grad))
```

```python
import math

import jax
import jax.numpy as jnp
from jax import lax
from jax.experimental import pallas as pl
from jax.experimental.pallas import tpu as pltpu
from jax.sharding import PartitionSpec as P

BF = jnp.bfloat16
F32 = jnp.float32
SLABS = 4
LAG = 3
VMEM = 16 * 2**20


def mm(left, right, ldim, rdim):
    return lax.dot_general(
        left, right, (((ldim,), (rdim,)), ((), ())), preferred_element_type=F32
    )


def params():
    return pltpu.CompilerParams(vmem_limit_bytes=VMEM)


def partial_kernel(x_ref, c_ref, wg_ref, wu_ref, wd_ref, *refs):
    p_ref, s_ref = refs[-2:]
    x = x_ref[...]
    for i, part in enumerate(
        (
            mm(x, wg_ref[...], 1, 0),
            mm(x, wu_ref[...], 1, 0),
            mm(c_ref[...], wd_ref[...], 1, 1),
        )
    ):
        p_ref[i] = part
        s_ref[i] = part.astype(s_ref.dtype)


def partials(x, c, w_gate, w_up, w_down, h, slab, wire, behind):
    m, feat = x.shape
    bn = min(256, slab)
    nb = slab // bn
    cols = pl.BlockSpec((feat, bn), lambda j: (0, h * nb + j))
    whole = pl.BlockSpec((m, feat), lambda j: (0, 0))
    out = pl.BlockSpec((3, m, bn), lambda j: (0, 0, j))
    return pl.pallas_call(
        partial_kernel,
        grid=(nb,),
        in_specs=[
            whole,
            whole,
            cols,
            cols,
            pl.BlockSpec((bn, feat), lambda j: (h * nb + j, 0)),
        ]
        + [pl.BlockSpec(memory_space=pl.ANY)] * len(behind),
        out_specs=[out, out],
        out_shape=[
            jax.ShapeDtypeStruct((3, m, slab), F32),
            jax.ShapeDtypeStruct((3, m, slab), wire),
        ],
        compiler_params=params(),
        cost_estimate=pl.CostEstimate(
            flops=6 * m * feat * slab,
            bytes_accessed=6 * feat * slab + 18 * m * slab,
            transcendentals=0,
        ),
        name="partials",
    )(x, c, w_gate, w_up, w_down, *behind)


def grads_kernel(n, xt_ref, c_ref, *refs):
    fulls = refs[:n]
    gate_ref, up_ref, down_ref, mark_ref = refs[-4:]
    mark_ref[...] = jnp.zeros_like(mark_ref)
    hidden, gate_delta, up_delta = [
        jnp.concatenate([f[i] for f in fulls], 0) for i in range(3)
    ]
    gate_ref[...] = mm(xt_ref[...], gate_delta, 1, 0)
    up_ref[...] = mm(xt_ref[...], up_delta, 1, 0)
    down_ref[...] = mm(hidden, c_ref[...], 0, 0)


def weight_grads(xt, c, fulls, h, hid, before):
    feat, tok = xt.shape
    slab = fulls[0].shape[2]
    rows = fulls[0].shape[1]
    bn = min(256, slab)
    nb = slab // bn
    n = len(fulls)
    cols = pl.BlockSpec((feat, bn), lambda j: (0, h * nb + j))
    return pl.pallas_call(
        lambda *refs: grads_kernel(n, *refs),
        grid=(nb,),
        in_specs=[
            pl.BlockSpec((feat, tok), lambda j: (0, 0)),
            pl.BlockSpec((tok, feat), lambda j: (0, 0)),
        ]
        + [pl.BlockSpec((3, rows, bn), lambda j: (0, 0, j))] * n
        + [pl.BlockSpec(memory_space=pl.ANY)] * len(before),
        out_specs=[
            cols,
            cols,
            pl.BlockSpec((bn, feat), lambda j: (h * nb + j, 0)),
            pl.BlockSpec((8, 128), lambda j: (0, 0)),
        ],
        out_shape=[
            jax.ShapeDtypeStruct((feat, hid), F32),
            jax.ShapeDtypeStruct((feat, hid), F32),
            jax.ShapeDtypeStruct((hid, feat), F32),
            jax.ShapeDtypeStruct((8, 128), F32),
        ],
        input_output_aliases={2 + n + i: i for i in range(len(before))},
        compiler_params=params(),
        cost_estimate=pl.CostEstimate(
            flops=6 * tok * feat * slab,
            bytes_accessed=12 * feat * slab,
            transcendentals=0,
        ),
        name="weight_grads",
    )(xt, c, *fulls, *before)


HERE = pl.BlockSpec(memory_space=pltpu.VMEM)
FLAG = pl.BlockSpec(memory_space=pltpu.SMEM)
REST = pl.BlockSpec(memory_space=pl.ANY)


def results_of(gate, up, hidden_grad):
    sigma = jax.nn.sigmoid(gate)
    activated = gate * sigma
    return (
        (activated * up).astype(BF),
        (hidden_grad * up * sigma * (1.0 + gate * (1.0 - sigma))).astype(BF),
        (hidden_grad * activated).astype(BF),
    )


def small(kernel, name, shapes, args, flags=(), behind=()):
    n = len(flags) + len(args)
    m = n + len(behind)
    size = sum(math.prod(a.shape) * a.dtype.itemsize for a in list(args) + list(shapes))
    return pl.pallas_call(
        lambda *refs: kernel(*refs[:n], *refs[m:]),
        in_specs=[FLAG] * len(flags) + [HERE] * len(args) + [REST] * len(behind),
        out_specs=[HERE] * len(shapes),
        out_shape=list(shapes),
        compiler_params=params(),
        cost_estimate=pl.CostEstimate(flops=size, bytes_accessed=size, transcendentals=0),
        name=name,
    )(*flags, *args, *behind)


def halve(came, part, start, rows, wire):
    def kernel(came_ref, part_ref, send_ref, keep_ref):
        keep_ref[...] = came_ref[:, :rows].astype(F32) + part_ref[:, start : start + rows]
        send_ref[...] = (
            came_ref[:, rows:].astype(F32) + part_ref[:, start + rows : start + 2 * rows]
        ).astype(wire)

    shape = (3, rows, came.shape[2])
    return small(
        kernel,
        "halve",
        [jax.ShapeDtypeStruct(shape, wire), jax.ShapeDtypeStruct(shape, F32)],
        [came, part],
    )


def finish(keep, half, behind):
    def kernel(keep_ref, half_ref, done_ref):
        own = [keep_ref[i] + half_ref[i].astype(F32) for i in range(3)]
        for i, values in enumerate(results_of(*own)):
            done_ref[i] = values

    return small(
        kernel, "finish", [jax.ShapeDtypeStruct(keep.shape, BF)], [keep, half], (), behind
    )[0]


def choose(is_end, at_end, start, done, half, behind):
    rows = done.shape[1]

    def kernel(flag_ref, end_ref, done_ref, half_ref, out_ref):
        @pl.when(flag_ref[0] == 1)
        def _():
            out_ref[...] = end_ref[:, start : start + 2 * rows]

        @pl.when(flag_ref[0] == 0)
        def _():
            out_ref[:, :rows] = done_ref[...]
            out_ref[:, rows:] = half_ref[...]

    shape = jax.ShapeDtypeStruct((3, 2 * rows, done.shape[2]), BF)
    return small(
        kernel, "choose", [shape], [at_end, done, half], [is_end], behind
    )[0]


def body(tokens, gate_weight, up_weight, down_weight, cotangent):
    count = lax.axis_size("row")
    side = math.isqrt(count)
    place = lax.axis_index("row")
    across = place % side
    down = place // side
    core = across % 2
    upper = (down >= side // 2).astype(jnp.int32)
    groups = side // 2
    mid = side // 2
    wire = BF if side <= 4 else F32

    w_gate = gate_weight[0]
    w_up = up_weight[0]
    w_down = down_weight[0]
    hid = w_gate.shape[1]
    rows = tokens.shape[1]
    slab = hid // SLABS

    def swap(values, bits):
        return lax.ppermute(values, "row", [(i, i ^ bits) for i in range(count)])

    def along(values, moves):
        route = [
            (src * side + i, dst * side + i) for src, dst in moves for i in range(side)
        ]
        return lax.ppermute(values, "row", route)

    def middle(values):
        route = []
        for d in range(side):
            for i in range(side):
                to = (side - 1 - d, i) if d in (mid - 1, mid) else (d, i ^ 1)
                route.append((d * side + i, to[0] * side + to[1]))
        return lax.ppermute(values, "row", route)

    first = core == upper

    def pair(own):
        other = swap(own, 1)
        return jnp.where(
            first, jnp.concatenate([own, other], 0), jnp.concatenate([other, own], 0)
        )

    x_own, c_own = pair(tokens[0]), pair(cotangent[0])
    order = [(0, 0), (0, 1)] + [(g, h) for h in (0, 1) for g in range(1, groups)]
    for h in range(2, SLABS):
        order += [(g, h) for g in reversed(range(groups))]
    sums, sends = {}, {}
    inputs = {0: (x_own, c_own)}

    def prepare(gs, h, *behind):
        x, c = inputs[gs[0]] if len(gs) == 1 else inputs["all"]
        p, s = partials(x, c, w_gate, w_up, w_down, h, slab, wire, behind)
        for n, g in enumerate(gs):
            sums[g, h], sends[g, h] = (p, 2 * rows * n), (s, 2 * rows * n)

    def rows_of(entry):
        values, start = entry
        return lax.slice_in_dim(values, start, start + 2 * rows, axis=1)

    prepare([0], 0)
    for g in range(1, groups):
        inputs[g] = swap(x_own, 2 * g), swap(c_own, 2 * g)
    x_all, c_all = [
        jnp.concatenate([inputs[g][i] for g in range(groups)], 0) for i in range(2)
    ]
    inputs["all"] = x_all, c_all
    xt_all = x_all.T

    fulls = {}
    outs = [None] * groups
    grads = ()
    marks = []

    def settle(g, h, full):
        nonlocal grads
        fulls[g, h] = full
        lo = h * slab
        wg = lax.slice_in_dim(w_gate, lo, lo + slab, axis=1)
        wu = lax.slice_in_dim(w_up, lo, lo + slab, axis=1)
        wd = lax.slice_in_dim(w_down, lo, lo + slab, axis=0)
        step = (mm(full[0], wd, 1, 0), mm(full[1], wg, 1, 1) + mm(full[2], wu, 1, 1))
        outs[g] = step if outs[g] is None else (outs[g][0] + step[0], outs[g][1] + step[1])
        marks.extend(outs[g])
        if all((i, h) in fulls for i in range(groups)):
            *grads, mark = weight_grads(
                xt_all, c_all, [fulls[i, h] for i in range(groups)], h, hid, grads
            )
            marks.append(mark)

    if mid == 2:
        pairs = [(d, d ^ 1) for d in range(side)]
        is_end = ((down == 0) | (down == side - 1)).astype(jnp.int32).reshape(1)
        steps = len(order)
        made = {1: [([0], 1)]}
        made[2] = [([g], h) for h in (0, 1) for g in range(1, groups)]
        for h in range(2, SLABS):
            made[3 + 2 * (h - 2)] = [(list(range(groups)), h)]
        arrived, results = {}, {}

        def depart(t, *behind):
            if t < LAG:
                load = rows_of(sends[order[t]])
            elif t < steps:
                load = choose(is_end, *sends[order[t]], *results[t - LAG], behind)
            else:
                load = choose(is_end, *sends[order[-1]], *results[t - LAG], behind)
            arrived[t] = along(load, pairs)
            return load

        depart(0)
        prepare([0], 1, sends[0, 0][0])
        load = depart(1)
        for t in range(steps + LAG):
            came = arrived[t]
            marks.clear()
            behind = []
            if t < steps:
                send, keep = halve(came, *sums[order[t]], rows, wire)
                half = middle(send)
                behind = [send]
            for gs, h in made.get(t + 2, ()):
                prepare(gs, h, *(behind or [came]))
                marks.append(sends[gs[0], h][0])
            if t >= LAG:
                settle(*order[t - LAG], choose(is_end, came, 0, *results[t - LAG], behind))
            if t + 2 < steps + LAG:
                load = depart(t + 2, *marks)
            if t < steps:
                done = finish(keep, half, [load])
                results[t] = done, middle(done)
    else:
        prepare([0], 1)
        for g in range(1, groups):
            for h in (0, 1):
                prepare([g], h)
        for h in range(2, SLABS):
            prepare(list(range(groups)), h)
        for g, h in order:
            total = rows_of(sums[g, h])
            for r in range(mid - 1):
                moves = [(r, r + 1), (side - 1 - r, side - 2 - r)]
                total = total + along(total.astype(wire), moves).astype(F32)
            half = middle(total[:, rows:].astype(wire))
            done = jnp.stack(results_of(*(total[:, :rows] + half.astype(F32))))
            full = jnp.concatenate([done, middle(done)], 1)
            for r in reversed(range(mid - 1)):
                came = along(full, [(r + 1, r), (side - 2 - r, side - 1 - r)])
                full = jnp.where((down == r) | (down == side - 1 - r), came, full)
            settle(g, h, full)

    def core_sum(values):
        lower, higher = values[:rows], values[rows:]
        keep = jnp.where(first, lower, higher)
        send = jnp.where(first, higher, lower)
        return keep + swap(send, 1)

    mixed_grad = []
    for i in range(2):
        result = None
        for g in reversed(range(groups)):
            summed = core_sum(outs[g][i])
            if g > 0:
                summed = swap(summed, 2 * g)
            result = summed if result is None else result + summed
        mixed_grad.append(result.astype(BF)[None])
    return tuple(mixed_grad) + tuple(g[None] for g in grads)


def solution(mesh):
    spec = P(("groups", "row"), None, None)
    weight = P("row", None, None)
    return jax.shard_map(
        body,
        mesh=mesh,
        in_specs=(spec, weight, weight, weight, spec),
        out_specs=(spec,) * 5,
        check_vma=False,
    )
```

```python
import math

import jax
import jax.numpy as jnp
from jax import lax
from jax.experimental import pallas as pl
from jax.experimental.pallas import tpu as pltpu
from jax.sharding import PartitionSpec as P

BF = jnp.bfloat16
F32 = jnp.float32
SLABS = 4
LAG = 3
MIB = 2**20


def mm(left, right, ldim, rdim):
    return lax.dot_general(
        left, right, (((ldim,), (rdim,)), ((), ())), preferred_element_type=F32
    )


def params(mib):
    return pltpu.CompilerParams(vmem_limit_bytes=mib * MIB)


def partial_kernel(x_ref, c_ref, wg_ref, wu_ref, wd_ref, *refs):
    p_ref, s_ref = refs[-2:]
    x = x_ref[...]
    for i, part in enumerate(
        (
            mm(x, wg_ref[...], 1, 0),
            mm(x, wu_ref[...], 1, 0),
            mm(c_ref[...], wd_ref[...], 1, 1),
        )
    ):
        p_ref[i] = part
        s_ref[i] = part.astype(s_ref.dtype)


def partials(x, c, w_gate, w_up, w_down, h, slab, wire, behind):
    m, feat = x.shape
    bn = min(256, slab)
    nb = slab // bn
    cols = pl.BlockSpec((feat, bn), lambda j: (0, h * nb + j))
    whole = pl.BlockSpec((m, feat), lambda j: (0, 0))
    out = pl.BlockSpec((3, m, bn), lambda j: (0, 0, j))
    return pl.pallas_call(
        partial_kernel,
        grid=(nb,),
        in_specs=[
            whole,
            whole,
            cols,
            cols,
            pl.BlockSpec((bn, feat), lambda j: (h * nb + j, 0)),
        ]
        + [pl.BlockSpec(memory_space=pl.ANY)] * len(behind),
        out_specs=[out, out],
        out_shape=[
            in_vmem((3, m, slab), F32),
            in_vmem((3, m, slab), wire),
        ],
        compiler_params=params(14),
        cost_estimate=pl.CostEstimate(
            flops=6 * m * feat * slab,
            bytes_accessed=6 * feat * slab + 18 * m * slab,
            transcendentals=0,
        ),
        name="partials",
    )(x, c, w_gate, w_up, w_down, *behind)


def grads_kernel(n, xt_ref, c_ref, *refs):
    fulls = refs[:n]
    gate_ref, up_ref, down_ref, mark_ref = refs[-4:]
    mark_ref[...] = jnp.zeros_like(mark_ref)
    hidden, gate_delta, up_delta = [
        jnp.concatenate([f[i] for f in fulls], 0) for i in range(3)
    ]
    gate_ref[...] = mm(xt_ref[...], gate_delta, 1, 0)
    up_ref[...] = mm(xt_ref[...], up_delta, 1, 0)
    down_ref[...] = mm(hidden, c_ref[...], 0, 0)


def weight_grads(xt, c, fulls, h, hid, before):
    feat, tok = xt.shape
    slab = fulls[0].shape[2]
    rows = fulls[0].shape[1]
    bn = min(256, slab)
    nb = slab // bn
    n = len(fulls)
    cols = pl.BlockSpec((feat, bn), lambda j: (0, h * nb + j))
    return pl.pallas_call(
        lambda *refs: grads_kernel(n, *refs),
        grid=(nb,),
        in_specs=[
            pl.BlockSpec((feat, tok), lambda j: (0, 0)),
            pl.BlockSpec((tok, feat), lambda j: (0, 0)),
        ]
        + [pl.BlockSpec((3, rows, bn), lambda j: (0, 0, j))] * n
        + [pl.BlockSpec(memory_space=pl.ANY)] * len(before),
        out_specs=[
            cols,
            cols,
            pl.BlockSpec((bn, feat), lambda j: (h * nb + j, 0)),
            pl.BlockSpec((8, 128), lambda j: (0, 0)),
        ],
        out_shape=[
            jax.ShapeDtypeStruct((feat, hid), F32),
            jax.ShapeDtypeStruct((feat, hid), F32),
            jax.ShapeDtypeStruct((hid, feat), F32),
            jax.ShapeDtypeStruct((8, 128), F32),
        ],
        input_output_aliases={2 + n + i: i for i in range(len(before))},
        compiler_params=params(16),
        cost_estimate=pl.CostEstimate(
            flops=6 * tok * feat * slab,
            bytes_accessed=12 * feat * slab,
            transcendentals=0,
        ),
        name="weight_grads",
    )(xt, c, *fulls, *before)


def in_hbm(values):
    return pltpu.with_memory_space_constraint(values, pltpu.HBM)


def in_vmem(shape, dtype):
    return pltpu.VMEM(shape, dtype)


HERE = pl.BlockSpec(memory_space=pltpu.VMEM)
FLAG = pl.BlockSpec(memory_space=pltpu.SMEM)
REST = pl.BlockSpec(memory_space=pl.ANY)


def results_of(gate, up, hidden_grad):
    sigma = jax.nn.sigmoid(gate)
    activated = gate * sigma
    return (
        (activated * up).astype(BF),
        (hidden_grad * up * sigma * (1.0 + gate * (1.0 - sigma))).astype(BF),
        (hidden_grad * activated).astype(BF),
    )


def small(kernel, name, shapes, args, flags=(), behind=(), mib=4, spec=HERE):
    n = len(flags) + len(args)
    m = n + len(behind)
    size = sum(math.prod(a.shape) * 2 for a in list(args) + list(shapes))
    return pl.pallas_call(
        lambda *refs: kernel(*refs[:n], *refs[m:]),
        in_specs=[FLAG] * len(flags) + [spec] * len(args) + [REST] * len(behind),
        out_specs=[HERE] * len(shapes),
        out_shape=list(shapes),
        compiler_params=params(mib),
        cost_estimate=pl.CostEstimate(flops=size, bytes_accessed=size, transcendentals=0),
        name=name,
    )(*flags, *args, *behind)


def halve(came, part, start, rows, wire, behind):
    def kernel(came_ref, part_ref, send_ref, keep_ref):
        keep_ref[...] = came_ref[:, :rows].astype(F32) + part_ref[:, start : start + rows]
        send_ref[...] = (
            came_ref[:, rows:].astype(F32) + part_ref[:, start + rows : start + 2 * rows]
        ).astype(wire)

    shape = (3, rows, came.shape[2])
    return small(
        kernel,
        "halve",
        [in_vmem(shape, wire), in_vmem(shape, F32)],
        [came, part],
        (),
        behind,
    )


def finish(keep, half, behind):
    def kernel(keep_ref, half_ref, done_ref):
        own = [keep_ref[i] + half_ref[i].astype(F32) for i in range(3)]
        for i, values in enumerate(results_of(*own)):
            done_ref[i] = values

    return small(
        kernel, "finish", [in_vmem(keep.shape, BF)], [keep, half], (), behind
    )[0]


def stage(blocks, behind=()):
    n = len(blocks)
    m = n + len(behind)

    def kernel(*refs):
        copies = [
            pltpu.make_async_copy(refs[i], refs[m + i], refs[-1].at[i]) for i in range(n)
        ]
        for copy in copies:
            copy.start()
        for copy in copies:
            copy.wait()

    size = sum(math.prod(b.shape) * 2 for b in blocks)
    return pl.pallas_call(
        kernel,
        in_specs=[REST] * m,
        out_specs=[HERE] * n,
        out_shape=[in_vmem(b.shape, b.dtype) for b in blocks],
        scratch_shapes=[pltpu.SemaphoreType.DMA((n,))],
        compiler_params=params(4),
        cost_estimate=pl.CostEstimate(flops=size, bytes_accessed=size, transcendentals=0),
        name="stage",
    )(*[in_hbm(b) for b in blocks], *behind)


def gather(pairs):
    n = len(pairs)
    rows, feat = pairs[0][0].shape

    def kernel(*refs):
        x_ref, c_ref, xt_ref = refs[2 * n :]
        for i in range(n):
            cut = slice(i * rows, (i + 1) * rows)
            x_ref[cut] = refs[i][...]
            c_ref[cut] = refs[n + i][...]
            xt_ref[:, cut] = refs[i][...].T

    tok = n * rows
    return small(
        kernel,
        "gather",
        [in_vmem((tok, feat), BF), in_vmem((tok, feat), BF), in_vmem((feat, tok), BF)],
        [p[0] for p in pairs] + [p[1] for p in pairs],
        mib=8,
    )


def pair(flags, blocks):
    rows, feat = blocks[0].shape

    def kernel(flag_ref, *refs):
        for a_ref, b_ref, out_ref in (refs[0:2] + refs[4:5], refs[2:4] + refs[5:6]):

            @pl.when(flag_ref[0] % 2 == 0)
            def _():
                out_ref[:rows] = a_ref[...]
                out_ref[rows:] = b_ref[...]

            @pl.when(flag_ref[0] % 2 == 1)
            def _():
                out_ref[:rows] = b_ref[...]
                out_ref[rows:] = a_ref[...]

    return small(kernel, "pair", [in_vmem((2 * rows, feat), BF)] * 2, blocks, [flags])


def split(flags, values):
    rows, feat = values.shape[0] // 2, values.shape[1]

    def kernel(flag_ref, in_ref, send_ref, keep_ref):
        for flag in range(2):

            @pl.when(flag_ref[0] % 2 == flag)
            def _():
                keep_ref[...] = in_ref[flag * rows : (flag + 1) * rows]
                send_ref[...] = in_ref[(1 - flag) * rows : (2 - flag) * rows]

    return small(kernel, "split", [in_vmem((rows, feat), F32)] * 2, [values], [flags])


def choose(flags, at_end, start, done, half, behind):
    rows = done.shape[1]

    def kernel(flag_ref, end_ref, done_ref, half_ref, out_ref):
        @pl.when(flag_ref[0] >= 2)
        def _():
            out_ref[...] = end_ref[:, start : start + 2 * rows]

        @pl.when(flag_ref[0] < 2)
        def _():
            out_ref[:, :rows] = done_ref[...]
            out_ref[:, rows:] = half_ref[...]

    shape = in_vmem((3, 2 * rows, done.shape[2]), BF)
    return small(
        kernel, "choose", [shape], [at_end, done, half], [flags], behind
    )[0]


def body(tokens, gate_weight, up_weight, down_weight, cotangent):
    count = lax.axis_size("row")
    side = math.isqrt(count)
    place = lax.axis_index("row")
    across = place % side
    down = place // side
    core = across % 2
    upper = (down >= side // 2).astype(jnp.int32)
    groups = side // 2
    mid = side // 2
    wire = BF if side <= 4 else F32

    w_gate = gate_weight[0]
    w_up = up_weight[0]
    w_down = down_weight[0]
    hid = w_gate.shape[1]
    rows = tokens.shape[1]
    slab = hid // SLABS

    def swap(values, bits):
        return lax.ppermute(values, "row", [(i, i ^ bits) for i in range(count)])

    def along(values, moves):
        route = [
            (src * side + i, dst * side + i) for src, dst in moves for i in range(side)
        ]
        return lax.ppermute(values, "row", route)

    def middle(values):
        route = []
        for d in range(side):
            for i in range(side):
                to = (side - 1 - d, i) if d in (mid - 1, mid) else (d, i ^ 1)
                route.append((d * side + i, to[0] * side + to[1]))
        return lax.ppermute(values, "row", route)

    is_end = ((down == 0) | (down == side - 1)).astype(jnp.int32)
    flags = ((core != upper).astype(jnp.int32) + 2 * is_end).reshape(1)

    x_mine, c_mine = stage([tokens[0], cotangent[0]])
    x_own, c_own = pair(
        flags,
        [x_mine, swap(tokens[0], 1), c_mine, swap(cotangent[0], 1)],
    )
    lead = SLABS // 2
    order = [(0, h) for h in range(lead)]
    order += [(g, h) for h in range(SLABS) for g in range(1, groups)]
    order += [(0, h) for h in range(lead, SLABS)]
    sums, sends = {}, {}
    inputs = {0: (x_own, c_own)}

    def prepare(gs, h, *behind):
        x, c = inputs[gs[0]] if len(gs) == 1 else inputs["all"]
        p, s = partials(x, c, *weights, h, slab, wire, behind)
        for n, g in enumerate(gs):
            sums[g, h], sends[g, h] = (p, 2 * rows * n), (s, 2 * rows * n)

    def rows_of(entry):
        values, start = entry
        return lax.slice_in_dim(values, start, start + 2 * rows, axis=1)

    weights = [in_hbm(w) for w in (w_gate, w_up, w_down)]
    prepare([0], 0)
    for g in range(1, groups):
        inputs[g] = swap(x_own, 2 * g), swap(c_own, 2 * g)
    x_all, c_all, xt_all = gather([inputs[g] for g in range(groups)])
    inputs["all"] = x_all, c_all

    def core_sum(values):
        send, keep = split(flags, values)
        return keep + swap(send, 1)

    fulls = {}
    received = [None, None]
    last = {}
    for g, h in order:
        last[g] = h
    outs = [None] * groups
    grads = ()
    marks = []

    def settle(g, h, full):
        nonlocal grads
        fulls[g, h] = full
        lo = h * slab
        wg = lax.slice_in_dim(w_gate, lo, lo + slab, axis=1)
        wu = lax.slice_in_dim(w_up, lo, lo + slab, axis=1)
        wd = lax.slice_in_dim(w_down, lo, lo + slab, axis=0)
        step = (mm(full[0], wd, 1, 0), mm(full[1], wg, 1, 1) + mm(full[2], wu, 1, 1))
        outs[g] = step if outs[g] is None else (outs[g][0] + step[0], outs[g][1] + step[1])
        marks.extend(outs[g])
        if g > 0 and h == last[g]:
            for i in range(2):
                came = swap(outs[g][i].astype(wire), 2 * g).astype(F32)
                received[i] = came if received[i] is None else received[i] + came
        if all((i, h) in fulls for i in range(groups)):
            *grads, mark = weight_grads(
                xt_all, c_all, [fulls[i, h] for i in range(groups)], h, hid, grads
            )
            marks.append(mark)

    if mid == 2:
        pairs = [(d, d ^ 1) for d in range(side)]
        steps = len(order)
        made = {t: [([g], h)] for t, (g, h) in enumerate(order) if h < lead}
        for h in range(lead, SLABS):
            made[order.index((1, h))] = [(list(range(groups)), h)]
        arrived, results = {}, {}

        def depart(t, *behind):
            if t < LAG:
                load = rows_of(sends[order[t]])
            elif t < steps:
                load = choose(flags, *sends[order[t]], *results[t - LAG], behind)
            else:
                load = choose(flags, *sends[order[-1]], *results[t - LAG], behind)
            arrived[t] = along(load, pairs)
            return load

        depart(0)
        prepare([0], 1, sends[0, 0][0])
        load = depart(1)
        w_gate, w_up, w_down = weights = stage([w_gate, w_up, w_down], [load])
        waiting = None
        for t in range(steps + LAG):
            came = arrived[t]
            marks.clear()
            behind = [load]
            started = None
            if t < steps:
                send, keep = halve(came, *sums[order[t]], rows, wire, behind)
                started = keep, middle(send)
                behind = [send]
            if waiting is not None:
                done = finish(*waiting, behind)
                results[t - 1] = done, middle(done)
                behind = [done]
            waiting = started
            for gs, h in made.get(t + 2, ()):
                prepare(gs, h, *behind)
                marks.append(sends[gs[0], h][0])
            if t >= LAG:
                settle(*order[t - LAG], choose(flags, came, 0, *results[t - LAG], behind))
            if t == steps - 1:
                done = finish(*waiting, marks)
                results[t] = done, middle(done)
                marks.append(done)
                waiting = None
            if t + 2 < steps + LAG:
                load = depart(t + 2, *marks)
    else:
        for h in range(lead):
            for g in range(groups):
                if g + h > 0:
                    prepare([g], h)
        for h in range(lead, SLABS):
            prepare(list(range(groups)), h)
        for g, h in order:
            total = rows_of(sums[g, h])
            for r in range(mid - 1):
                moves = [(r, r + 1), (side - 1 - r, side - 2 - r)]
                total = total + along(total.astype(wire), moves).astype(F32)
            half = middle(total[:, rows:].astype(wire))
            done = jnp.stack(results_of(*(total[:, :rows] + half.astype(F32))))
            full = jnp.concatenate([done, middle(done)], 1)
            for r in reversed(range(mid - 1)):
                came = along(full, [(r + 1, r), (side - 2 - r, side - 1 - r)])
                full = jnp.where((down == r) | (down == side - 1 - r), came, full)
            settle(g, h, full)

    return (
        tuple(core_sum(received[i] + outs[0][i]).astype(BF)[None] for i in range(2))
        + tuple(g[None] for g in grads)
    )


def solution(mesh):
    spec = P(("groups", "row"), None, None)
    weight = P("row", None, None)
    return jax.shard_map(
        body,
        mesh=mesh,
        in_specs=(spec, weight, weight, weight, spec),
        out_specs=(spec,) * 5,
        check_vma=False,
    )
```

```python
import math

import jax
import jax.numpy as jnp
from jax import lax
from jax.experimental import pallas as pl
from jax.experimental.pallas import tpu as pltpu
from jax.sharding import PartitionSpec as P

BF = jnp.bfloat16
F32 = jnp.float32
WIDE = 4
PIECES = 1
LAG = 3
LATE = 2
MIB = 2**20


def mm(left, right, ldim, rdim):
    return lax.dot_general(
        left, right, (((ldim,), (rdim,)), ((), ())), preferred_element_type=F32
    )


def params(mib):
    return pltpu.CompilerParams(vmem_limit_bytes=mib * MIB)


def partials(x, c, weights, chunks, width, wire, behind):
    m, feat = x.shape
    n = len(chunks)
    k = 5 + len(behind)

    def kernel(*refs):
        x_ref, c_ref, wg_ref, wu_ref, wd_ref = refs[:5]
        for j in range(n):

            @pl.when(pl.program_id(0) == j)
            def _():
                for i, part in enumerate(
                    (
                        mm(x_ref[...], wg_ref[...], 1, 0),
                        mm(x_ref[...], wu_ref[...], 1, 0),
                        mm(c_ref[...], wd_ref[...], 1, 1),
                    )
                ):
                    refs[k + j][i] = part
                    refs[k + n + j][i] = part.astype(wire)

    cols = pl.BlockSpec((feat, width), lambda j: (0, chunks[0] + j))
    whole = pl.BlockSpec((m, feat), lambda j: (0, 0))
    shape = (3, m, width)
    return pl.pallas_call(
        kernel,
        grid=(n,),
        in_specs=[whole, whole, cols, cols, pl.BlockSpec((width, feat), lambda j: (chunks[0] + j, 0))]
        + [REST] * len(behind),
        out_specs=[pl.BlockSpec(shape, lambda j: (0, 0, 0))] * (2 * n),
        out_shape=[in_vmem(shape, F32)] * n + [in_vmem(shape, wire)] * n,
        compiler_params=params(16),
        cost_estimate=pl.CostEstimate(
            flops=6 * m * feat * width * n,
            bytes_accessed=6 * feat * width * n,
            transcendentals=0,
        ),
        name="partials",
    )(x, c, *weights, *behind)


def grads_kernel(n, xt_ref, c_ref, *refs):
    fulls = refs[:n]
    gate_ref, up_ref, down_ref, mark_ref = refs[-4:]
    mark_ref[...] = jnp.zeros_like(mark_ref)
    hidden, gate_delta, up_delta = [
        jnp.concatenate([f[i] for f in fulls], 0) for i in range(3)
    ]
    gate_ref[...] = mm(xt_ref[...], gate_delta, 1, 0)
    up_ref[...] = mm(xt_ref[...], up_delta, 1, 0)
    down_ref[...] = mm(hidden, c_ref[...], 0, 0)


def weight_grads(xt, c, fulls, h, hid, before, behind):
    feat, tok = xt.shape
    slab = fulls[0].shape[2]
    rows = fulls[0].shape[1]
    bn = min(256, slab)
    nb = slab // bn
    n = len(fulls)
    cols = pl.BlockSpec((feat, bn), lambda j: (0, h * nb + j))
    return pl.pallas_call(
        lambda *refs: grads_kernel(n, *refs),
        grid=(nb,),
        in_specs=[
            pl.BlockSpec((feat, tok), lambda j: (0, 0)),
            pl.BlockSpec((tok, feat), lambda j: (0, 0)),
        ]
        + [pl.BlockSpec((3, rows, bn), lambda j: (0, 0, j))] * n
        + [REST] * (len(before) + len(behind)),
        out_specs=[
            cols,
            cols,
            pl.BlockSpec((bn, feat), lambda j: (h * nb + j, 0)),
            pl.BlockSpec((8, 128), lambda j: (0, 0)),
        ],
        out_shape=[
            jax.ShapeDtypeStruct((feat, hid), F32),
            jax.ShapeDtypeStruct((feat, hid), F32),
            jax.ShapeDtypeStruct((hid, feat), F32),
            jax.ShapeDtypeStruct((8, 128), F32),
        ],
        input_output_aliases={2 + n + i: i for i in range(len(before))},
        compiler_params=params(16),
        cost_estimate=pl.CostEstimate(
            flops=6 * tok * feat * slab,
            bytes_accessed=12 * feat * slab,
            transcendentals=0,
        ),
        name="weight_grads",
    )(xt, c, *fulls, *before, *behind)


def in_hbm(values):
    return pltpu.with_memory_space_constraint(values, pltpu.HBM)


def in_vmem(shape, dtype):
    return pltpu.VMEM(shape, dtype)


HERE = pl.BlockSpec(memory_space=pltpu.VMEM)
FLAG = pl.BlockSpec(memory_space=pltpu.SMEM)
REST = pl.BlockSpec(memory_space=pl.ANY)


def results_of(gate, up, hidden_grad):
    sigma = jax.nn.sigmoid(gate)
    activated = gate * sigma
    return (
        (activated * up).astype(BF),
        (hidden_grad * up * sigma * (1.0 + gate * (1.0 - sigma))).astype(BF),
        (hidden_grad * activated).astype(BF),
    )


def small(kernel, name, shapes, args, flags=(), behind=(), mib=4, spec=HERE):
    n = len(flags) + len(args)
    m = n + len(behind)
    size = sum(math.prod(a.shape) * 2 for a in list(args) + list(shapes))
    return pl.pallas_call(
        lambda *refs: kernel(*refs[:n], *refs[m:]),
        in_specs=[FLAG] * len(flags) + [spec] * len(args) + [REST] * len(behind),
        out_specs=[HERE] * len(shapes),
        out_shape=list(shapes),
        compiler_params=params(mib),
        cost_estimate=pl.CostEstimate(flops=size, bytes_accessed=size, transcendentals=0),
        name=name,
    )(*flags, *args, *behind)


def combine(came, part, start, rows, behind):
    def kernel(came_ref, part_ref, send_ref, keep_ref):
        total = came_ref[...].astype(F32) + part_ref[:, start : start + rows]
        keep_ref[...] = total
        send_ref[...] = total.astype(BF)

    shape = came.shape
    return small(
        kernel, "combine", [in_vmem(shape, BF), in_vmem(shape, F32)], [came, part], (), behind
    )


def finish(keep, came, behind):
    def kernel(keep_ref, came_ref, done_ref):
        own = [keep_ref[i] + came_ref[i].astype(F32) for i in range(3)]
        for i, values in enumerate(results_of(*own)):
            done_ref[i] = values

    return small(
        kernel, "finish", [in_vmem(keep.shape, BF)], [keep, came], (), behind
    )[0]


def stage(blocks, behind=()):
    n = len(blocks)
    m = n + len(behind)

    def kernel(*refs):
        copies = [
            pltpu.make_async_copy(refs[i], refs[m + i], refs[-1].at[i]) for i in range(n)
        ]
        for copy in copies:
            copy.start()
        for copy in copies:
            copy.wait()

    size = sum(math.prod(b.shape) * 2 for b in blocks)
    return pl.pallas_call(
        kernel,
        in_specs=[REST] * m,
        out_specs=[HERE] * n,
        out_shape=[in_vmem(b.shape, b.dtype) for b in blocks],
        scratch_shapes=[pltpu.SemaphoreType.DMA((n,))],
        compiler_params=params(4),
        cost_estimate=pl.CostEstimate(flops=size, bytes_accessed=size, transcendentals=0),
        name="stage",
    )(*[in_hbm(b) for b in blocks], *behind)


def gather(pairs):
    n = len(pairs)
    rows, feat = pairs[0][0].shape

    def kernel(*refs):
        x_ref, c_ref, xt_ref = refs[2 * n :]
        for i in range(n):
            cut = slice(i * rows, (i + 1) * rows)
            x_ref[cut] = refs[i][...]
            c_ref[cut] = refs[n + i][...]
            xt_ref[:, cut] = refs[i][...].T

    tok = n * rows
    return small(
        kernel,
        "gather",
        [in_vmem((tok, feat), BF), in_vmem((tok, feat), BF), in_vmem((feat, tok), BF)],
        [p[0] for p in pairs] + [p[1] for p in pairs],
        mib=8,
    )


def pair(flags, blocks):
    rows, feat = blocks[0].shape

    def kernel(flag_ref, *refs):
        for a_ref, b_ref, out_ref in (refs[0:2] + refs[4:5], refs[2:4] + refs[5:6]):

            @pl.when(flag_ref[0] % 2 == 0)
            def _():
                out_ref[:rows] = a_ref[...]
                out_ref[rows:] = b_ref[...]

            @pl.when(flag_ref[0] % 2 == 1)
            def _():
                out_ref[:rows] = b_ref[...]
                out_ref[rows:] = a_ref[...]

    return small(kernel, "pair", [in_vmem((2 * rows, feat), BF)] * 2, blocks, [flags])


def split(flags, values):
    rows, feat = values.shape[0] // 2, values.shape[1]

    def kernel(flag_ref, in_ref, send_ref, keep_ref):
        for flag in range(2):

            @pl.when(flag_ref[0] % 2 == flag)
            def _():
                keep_ref[...] = in_ref[flag * rows : (flag + 1) * rows]
                send_ref[...] = in_ref[(1 - flag) * rows : (2 - flag) * rows]

    return small(kernel, "split", [in_vmem((rows, feat), F32)] * 2, [values], [flags])


def choose(flags, at_end, start, done, behind):
    rows, width = done[0].shape[1:]
    n = len(at_end)

    def kernel(flag_ref, *refs):
        for j in range(n):
            cols = slice(j * width, (j + 1) * width)

            @pl.when(flag_ref[0] >= 2)
            def _():
                refs[-1][:, :, cols] = refs[j][:, start : start + rows]

            @pl.when(flag_ref[0] < 2)
            def _():
                refs[-1][:, :, cols] = refs[n + j][...]

    shape = in_vmem((3, rows, n * width), BF)
    return small(kernel, "choose", [shape], [*at_end, *done], [flags], behind)[0]


def body(tokens, gate_weight, up_weight, down_weight, cotangent):
    count = lax.axis_size("row")
    side = math.isqrt(count)
    place = lax.axis_index("row")
    across = place % side
    down = place // side
    core = across % 2
    groups = side // 2
    mid = side // 2
    wire = BF if side <= 4 else F32

    w_gate = gate_weight[0]
    w_up = up_weight[0]
    w_down = down_weight[0]
    hid = w_gate.shape[1]
    rows = tokens.shape[1]
    total_chunks = WIDE * PIECES
    width = hid // total_chunks

    def swap(values, bits):
        return lax.ppermute(values, "row", [(i, i ^ bits) for i in range(count)])

    def along(values, moves):
        route = [
            (src * side + i, dst * side + i) for src, dst in moves for i in range(side)
        ]
        return lax.ppermute(values, "row", route)

    def middle(values):
        route = []
        for d in range(side):
            for i in range(side):
                to = (side - 1 - d, i) if d in (mid - 1, mid) else (d, i ^ 1)
                route.append((d * side + i, to[0] * side + to[1]))
        return lax.ppermute(values, "row", route)

    is_end = ((down == 0) | (down == side - 1)).astype(jnp.int32)
    flags = (core + 2 * is_end).reshape(1)

    x_mine, c_mine = stage([tokens[0], cotangent[0]])
    x_own, c_own = pair(
        flags,
        [x_mine, swap(tokens[0], 1), c_mine, swap(cotangent[0], 1)],
    )
    last = total_chunks - PIECES * LATE
    order = [(0, c) for c in range(last)]
    order += [(g, c) for g in range(1, groups) for c in range(total_chunks)]
    order += [(0, c) for c in range(last, total_chunks)]
    sums, sends = {}, {}
    inputs = {0: (x_own, c_own)}

    weights = [in_hbm(w) for w in (w_gate, w_up, w_down)]

    def prepare(gs, chunks, *behind):
        x, c = inputs[gs[0]] if len(gs) == 1 else inputs["all"]
        made = partials(x, c, weights, chunks, width, wire, behind)
        for j, chunk in enumerate(chunks):
            for n, g in enumerate(gs):
                sums[g, chunk] = made[j], 2 * rows * n
                sends[g, chunk] = made[len(chunks) + j], 2 * rows * n
        return made[0]

    def rows_of(entry):
        values, start = entry
        return lax.slice_in_dim(values, start, start + 2 * rows, axis=1)

    prepare([0], [0])
    for g in range(1, groups):
        inputs[g] = swap(x_own, 2 * g), swap(c_own, 2 * g)
    x_all, c_all, xt_all = gather([inputs[g] for g in range(groups)])
    inputs["all"] = x_all, c_all

    def core_sum(values):
        send, keep = split(flags, values)
        return keep + swap(send, 1)

    fulls = {}
    received = [None, None]
    outs = [None] * groups
    grads = ()
    marks = []

    def settle(g, h, full):
        fulls[g, h] = full
        lo, hi = h * PIECES * width, (h + 1) * PIECES * width
        wg = lax.slice_in_dim(w_gate, lo, hi, axis=1)
        wu = lax.slice_in_dim(w_up, lo, hi, axis=1)
        wd = lax.slice_in_dim(w_down, lo, hi, axis=0)
        step = (mm(full[0], wd, 1, 0), mm(full[1], wg, 1, 1) + mm(full[2], wu, 1, 1))
        outs[g] = step if outs[g] is None else (outs[g][0] + step[0], outs[g][1] + step[1])
        marks.extend(outs[g])
        if g > 0 and h == WIDE - 1:
            for i in range(2):
                came = swap(outs[g][i].astype(wire), 2 * g).astype(F32)
                received[i] = came if received[i] is None else received[i] + came

    def weigh(h, behind):
        nonlocal grads
        *grads, mark = weight_grads(
            xt_all, c_all, [fulls[g, h] for g in range(groups)], h, hid, grads, behind
        )
        marks.append(mark)

    if mid == 2:
        pairs = [(d, d ^ 1) for d in range(side)]
        steps = len(order)
        step_of = {key: t for t, key in enumerate(order)}
        made = {}
        for c in range(PIECES, last, PIECES):
            made.setdefault(step_of[0, c] - 3, []).append(([0], range(c, c + PIECES)))
        for c in range(0, last, PIECES):
            made.setdefault(step_of[1, c] - 3 + (c == 0), []).append(([1], range(c, c + PIECES)))
        for c in range(last, total_chunks, PIECES):
            made.setdefault(step_of[1, c] - 3, []).append(([0, 1], range(c, c + PIECES)))
        arrived, results = {}, {}

        def depart(t, *behind):
            if t < LAG:
                load = rows_of(sends[order[t]])
            else:
                at_end, start = sends[order[min(t, steps - 1)]]
                load = choose(flags, [at_end], start, [results[t - LAG]], behind)
            arrived[t] = along(load, pairs)
            return load

        depart(0)
        last_made = sends[0, 0][0]
        if PIECES > 1:
            last_made = prepare([0], [1], last_made)
        for t in (-2, -1):
            for gs, chunks in made.get(t, ()):
                last_made = prepare(gs, list(chunks), last_made)
            if t == -2:
                depart(1)
        behind = [last_made]
        staged = []
        waiting = None
        ready = []
        for t in range(steps + LAG):
            started = None
            if t < steps:
                send, keep = combine(arrived[t], *sums[order[t]], 2 * rows, behind)
                started = keep, middle(send)
                behind = [send]
            if waiting is not None:
                results[t - 1] = finish(*waiting, behind)
                behind = [results[t - 1]]
            waiting = started
            for gs, chunks in made.get(t, ()):
                behind = [prepare(gs, list(chunks), *behind)]
            if t + 2 < steps + LAG:
                load = depart(t + 2, *behind)
                if t + 2 >= LAG:
                    behind = [load]
            if t < 3:
                staged += stage([(w_gate, w_up, w_down)[t]], behind)
                behind = staged[-1:]
                if t == 2:
                    w_gate, w_up, w_down = weights = staged
            if t >= LAG:
                g, c = order[t - LAG]
                if c % PIECES == PIECES - 1:
                    past = range(t - LAG - PIECES + 1, t - LAG + 1)
                    done = [results[u] for u in past]
                    came = [arrived[u + LAG] for u in past]
                    marks.clear()
                    settle(g, c // PIECES, choose(flags, came, 0, done, behind))
                    behind = list(marks)
            for h in range(WIDE - 1):
                if h not in ready and all((i, h) in fulls for i in range(groups)):
                    ready.append(h)
                    marks.clear()
                    weigh(h, behind)
                    behind = list(marks)
        weigh(WIDE - 1, [])
    else:
        for g in range(groups):
            for h in range(WIDE):
                chunks = [h * PIECES + j for j in range(PIECES)]
                chunks = [c for c in chunks if (g, c) not in sums]
                if chunks:
                    prepare([g], chunks)
                pieces = []
                for c in range(h * PIECES, (h + 1) * PIECES):
                    total = rows_of(sums[g, c])
                    for r in range(mid - 1):
                        moves = [(r, r + 1), (side - 1 - r, side - 2 - r)]
                        total = total + along(total.astype(wire), moves).astype(F32)
                    total = total + middle(total.astype(wire)).astype(F32)
                    full = jnp.stack(results_of(*total))
                    for r in reversed(range(mid - 1)):
                        came = along(full, [(r + 1, r), (side - 2 - r, side - 1 - r)])
                        full = jnp.where((down == r) | (down == side - 1 - r), came, full)
                    pieces.append(full)
                settle(g, h, jnp.concatenate(pieces, 2))
        for h in range(WIDE):
            weigh(h, [])

    return (
        tuple(core_sum(received[i] + outs[0][i]).astype(BF)[None] for i in range(2))
        + tuple(g[None] for g in grads)
    )


def solution(mesh):
    spec = P(("groups", "row"), None, None)
    weight = P("row", None, None)
    return jax.shard_map(
        body,
        mesh=mesh,
        in_specs=(spec, weight, weight, weight, spec),
        out_specs=(spec,) * 5,
        check_vma=False,
    )
```

```python
import math

import jax
import jax.numpy as jnp
from jax import lax
from jax.experimental import pallas as pl
from jax.experimental.pallas import tpu as pltpu
from jax.sharding import PartitionSpec as P

BF = jnp.bfloat16
F32 = jnp.float32
WIDE = 4
PIECES = 1
LAG = 3
LATE = 2
MIB = 2**20


def mm(left, right, ldim, rdim):
    return lax.dot_general(
        left, right, (((ldim,), (rdim,)), ((), ())), preferred_element_type=F32
    )


def params(mib):
    return pltpu.CompilerParams(vmem_limit_bytes=mib * MIB)


def partials(x, c, weights, chunks, width, wire, behind):
    m, feat = x.shape
    n = len(chunks)
    k = 5 + len(behind)

    def kernel(*refs):
        x_ref, c_ref, wg_ref, wu_ref, wd_ref = refs[:5]
        for j in range(n):

            @pl.when(pl.program_id(0) == j)
            def _():
                for i, part in enumerate(
                    (
                        mm(x_ref[...], wg_ref[...], 1, 0),
                        mm(x_ref[...], wu_ref[...], 1, 0),
                        mm(c_ref[...], wd_ref[...], 1, 1),
                    )
                ):
                    refs[k + j][i] = part
                    refs[k + n + j][i] = part.astype(wire)

    cols = pl.BlockSpec((feat, width), lambda j: (0, chunks[0] + j))
    whole = pl.BlockSpec((m, feat), lambda j: (0, 0))
    shape = (3, m, width)
    return pl.pallas_call(
        kernel,
        grid=(n,),
        in_specs=[whole, whole, cols, cols, pl.BlockSpec((width, feat), lambda j: (chunks[0] + j, 0))]
        + [REST] * len(behind),
        out_specs=[pl.BlockSpec(shape, lambda j: (0, 0, 0))] * (2 * n),
        out_shape=[in_vmem(shape, F32)] * n + [in_vmem(shape, wire)] * n,
        compiler_params=params(16),
        cost_estimate=pl.CostEstimate(
            flops=6 * m * feat * width * n,
            bytes_accessed=6 * feat * width * n,
            transcendentals=0,
        ),
        name="partials",
    )(x, c, *weights, *behind)


def grads_kernel(n, xt_ref, c_ref, *refs):
    fulls = refs[:n]
    gate_ref, up_ref, down_ref, mark_ref = refs[-4:]
    mark_ref[...] = jnp.zeros_like(mark_ref)
    hidden, gate_delta, up_delta = [
        jnp.concatenate([f[i] for f in fulls], 0) for i in range(3)
    ]
    gate_ref[...] = mm(xt_ref[...], gate_delta, 1, 0)
    up_ref[...] = mm(xt_ref[...], up_delta, 1, 0)
    down_ref[...] = mm(hidden, c_ref[...], 0, 0)


def weight_grads(xt, c, fulls, h, hid, before, behind):
    feat, tok = xt.shape
    slab = fulls[0].shape[2]
    rows = fulls[0].shape[1]
    bn = min(256, slab)
    nb = slab // bn
    n = len(fulls)
    cols = pl.BlockSpec((feat, bn), lambda j: (0, h * nb + j))
    return pl.pallas_call(
        lambda *refs: grads_kernel(n, *refs),
        grid=(nb,),
        in_specs=[
            pl.BlockSpec((feat, tok), lambda j: (0, 0)),
            pl.BlockSpec((tok, feat), lambda j: (0, 0)),
        ]
        + [pl.BlockSpec((3, rows, bn), lambda j: (0, 0, j))] * n
        + [REST] * (len(before) + len(behind)),
        out_specs=[
            cols,
            cols,
            pl.BlockSpec((bn, feat), lambda j: (h * nb + j, 0)),
            pl.BlockSpec((8, 128), lambda j: (0, 0)),
        ],
        out_shape=[
            jax.ShapeDtypeStruct((feat, hid), F32),
            jax.ShapeDtypeStruct((feat, hid), F32),
            jax.ShapeDtypeStruct((hid, feat), F32),
            jax.ShapeDtypeStruct((8, 128), F32),
        ],
        input_output_aliases={2 + n + i: i for i in range(len(before))},
        compiler_params=params(16),
        cost_estimate=pl.CostEstimate(
            flops=6 * tok * feat * slab,
            bytes_accessed=12 * feat * slab,
            transcendentals=0,
        ),
        name="weight_grads",
    )(xt, c, *fulls, *before, *behind)


def in_hbm(values):
    return pltpu.with_memory_space_constraint(values, pltpu.HBM)


def in_vmem(shape, dtype):
    return pltpu.VMEM(shape, dtype)


HERE = pl.BlockSpec(memory_space=pltpu.VMEM)
FLAG = pl.BlockSpec(memory_space=pltpu.SMEM)
REST = pl.BlockSpec(memory_space=pl.ANY)


def results_of(gate, up, hidden_grad):
    sigma = jax.nn.sigmoid(gate)
    activated = gate * sigma
    return (
        (activated * up).astype(BF),
        (hidden_grad * up * sigma * (1.0 + gate * (1.0 - sigma))).astype(BF),
        (hidden_grad * activated).astype(BF),
    )


def small(kernel, name, shapes, args, flags=(), behind=(), mib=4, spec=HERE):
    n = len(flags) + len(args)
    m = n + len(behind)
    size = sum(math.prod(a.shape) * 2 for a in list(args) + list(shapes))
    return pl.pallas_call(
        lambda *refs: kernel(*refs[:n], *refs[m:]),
        in_specs=[FLAG] * len(flags) + [spec] * len(args) + [REST] * len(behind),
        out_specs=[HERE] * len(shapes),
        out_shape=list(shapes),
        compiler_params=params(mib),
        cost_estimate=pl.CostEstimate(flops=size, bytes_accessed=size, transcendentals=0),
        name=name,
    )(*flags, *args, *behind)


def combine(came, part, start, rows, behind):
    def kernel(came_ref, part_ref, send_ref, keep_ref):
        total = came_ref[...].astype(F32) + part_ref[:, start : start + rows]
        keep_ref[...] = total
        send_ref[...] = total.astype(BF)

    shape = came.shape
    return small(
        kernel, "combine", [in_vmem(shape, BF), in_vmem(shape, F32)], [came, part], (), behind
    )


def finish(keep, came, behind):
    def kernel(keep_ref, came_ref, done_ref):
        own = [keep_ref[i] + came_ref[i].astype(F32) for i in range(3)]
        for i, values in enumerate(results_of(*own)):
            done_ref[i] = values

    return small(
        kernel, "finish", [in_vmem(keep.shape, BF)], [keep, came], (), behind
    )[0]


def stage(pieces, behind=()):
    n = len(pieces)
    m = n + len(behind)
    shapes = [shape for _, shape in pieces]
    cuts = [max(1, shape[0] // 256) for shape in shapes]

    def kernel(*refs):
        sems = refs[-1]
        copies = []
        for i, shape in enumerate(shapes):
            size = shape[0] // cuts[i]
            for j in range(cuts[i]):
                part = pl.ds(j * size, size)
                copies.append(
                    pltpu.make_async_copy(
                        refs[i].at[part, pl.ds(0, shape[1])],
                        refs[m + i].at[part],
                        sems.at[len(copies)],
                    )
                )
        for copy in copies:
            copy.start()
        for copy in copies:
            copy.wait()

    size = sum(math.prod(shape) * 2 for shape in shapes)
    return pl.pallas_call(
        kernel,
        in_specs=[REST] * m,
        out_specs=[HERE] * n,
        out_shape=[in_vmem(shape, BF) for shape in shapes],
        scratch_shapes=[pltpu.SemaphoreType.DMA((sum(cuts),))],
        compiler_params=params(4),
        cost_estimate=pl.CostEstimate(flops=size, bytes_accessed=size, transcendentals=0),
        name="stage",
    )(*[in_hbm(values) for values, _ in pieces], *behind)


def close(keeps, cames):
    n = len(keeps)

    def kernel(*refs):
        for i in range(n):
            refs[2 * n + i][...] = (refs[i][...] + refs[n + i][...]).astype(BF)

    shape = keeps[0].shape
    return pl.pallas_call(
        kernel,
        in_specs=[HERE] * (2 * n),
        out_shape=[jax.ShapeDtypeStruct(shape, BF)] * n,
        compiler_params=params(4),
        name="close",
    )(*keeps, *cames)


def gather(pairs):
    n = len(pairs)
    rows, feat = pairs[0][0].shape

    def kernel(*refs):
        x_ref, c_ref, xt_ref = refs[2 * n :]
        for i in range(n):
            cut = slice(i * rows, (i + 1) * rows)
            x_ref[cut] = refs[i][...]
            c_ref[cut] = refs[n + i][...]
            xt_ref[:, cut] = refs[i][...].T

    tok = n * rows
    return small(
        kernel,
        "gather",
        [in_vmem((tok, feat), BF), in_vmem((tok, feat), BF), in_vmem((feat, tok), BF)],
        [p[0] for p in pairs] + [p[1] for p in pairs],
        mib=8,
    )


def pair(flags, blocks):
    rows, feat = blocks[0].shape

    def kernel(flag_ref, *refs):
        for a_ref, b_ref, out_ref in (refs[0:2] + refs[4:5], refs[2:4] + refs[5:6]):

            @pl.when(flag_ref[0] % 2 == 0)
            def _():
                out_ref[:rows] = a_ref[...]
                out_ref[rows:] = b_ref[...]

            @pl.when(flag_ref[0] % 2 == 1)
            def _():
                out_ref[:rows] = b_ref[...]
                out_ref[rows:] = a_ref[...]

    return small(kernel, "pair", [in_vmem((2 * rows, feat), BF)] * 2, blocks, [flags])


def split(flags, values):
    rows, feat = values.shape[0] // 2, values.shape[1]

    def kernel(flag_ref, in_ref, send_ref, keep_ref):
        for flag in range(2):

            @pl.when(flag_ref[0] % 2 == flag)
            def _():
                keep_ref[...] = in_ref[flag * rows : (flag + 1) * rows]
                send_ref[...] = in_ref[(1 - flag) * rows : (2 - flag) * rows]

    return small(kernel, "split", [in_vmem((rows, feat), F32)] * 2, [values], [flags])


def choose(flags, at_end, start, done, behind):
    rows, width = done[0].shape[1:]
    n = len(at_end)

    def kernel(flag_ref, *refs):
        for j in range(n):
            cols = slice(j * width, (j + 1) * width)

            @pl.when(flag_ref[0] >= 2)
            def _():
                refs[-1][:, :, cols] = refs[j][:, start : start + rows]

            @pl.when(flag_ref[0] < 2)
            def _():
                refs[-1][:, :, cols] = refs[n + j][...]

    shape = in_vmem((3, rows, n * width), BF)
    return small(kernel, "choose", [shape], [*at_end, *done], [flags], behind)[0]


def body(tokens, gate_weight, up_weight, down_weight, cotangent):
    count = lax.axis_size("row")
    side = math.isqrt(count)
    place = lax.axis_index("row")
    across = place % side
    down = place // side
    core = across % 2
    groups = side // 2
    mid = side // 2
    wire = BF if side <= 4 else F32

    w_gate = gate_weight[0]
    w_up = up_weight[0]
    w_down = down_weight[0]
    hid = w_gate.shape[1]
    rows = tokens.shape[1]
    total_chunks = WIDE * PIECES
    width = hid // total_chunks

    def swap(values, bits):
        return lax.ppermute(values, "row", [(i, i ^ bits) for i in range(count)])

    def along(values, moves):
        route = [
            (src * side + i, dst * side + i) for src, dst in moves for i in range(side)
        ]
        return lax.ppermute(values, "row", route)

    def middle(values):
        route = []
        for d in range(side):
            for i in range(side):
                to = (side - 1 - d, i) if d in (mid - 1, mid) else (d, i ^ 1)
                route.append((d * side + i, to[0] * side + to[1]))
        return lax.ppermute(values, "row", route)

    is_end = ((down == 0) | (down == side - 1)).astype(jnp.int32)
    flags = (core + 2 * is_end).reshape(1)

    slab = width * PIECES
    feat = w_gate.shape[0]
    early = [(w_gate, (feat, slab)), (w_up, (feat, slab)), (w_down, (slab, feat))]
    x_mine, c_mine, *weights = stage(
        [(tokens[0], tokens.shape[1:]), (cotangent[0], tokens.shape[1:])] + early
    )
    x_own, c_own = pair(
        flags,
        [x_mine, swap(tokens[0], 1), c_mine, swap(cotangent[0], 1)],
    )
    last = total_chunks - PIECES * LATE
    order = [(0, c) for c in range(last)]
    order += [(g, c) for g in range(1, groups) for c in range(total_chunks)]
    order += [(0, c) for c in range(last, total_chunks)]
    sums, sends = {}, {}
    inputs = {0: (x_own, c_own)}

    def prepare(gs, chunks, *behind):
        x, c = inputs[gs[0]] if len(gs) == 1 else inputs["all"]
        made = partials(x, c, weights, chunks, width, wire, behind)
        for j, chunk in enumerate(chunks):
            for n, g in enumerate(gs):
                sums[g, chunk] = made[j], 2 * rows * n
                sends[g, chunk] = made[len(chunks) + j], 2 * rows * n
        return made[0]

    def rows_of(entry):
        values, start = entry
        return lax.slice_in_dim(values, start, start + 2 * rows, axis=1)

    prepare([0], [0])
    weights = [in_hbm(w) for w in (w_gate, w_up, w_down)]
    for g in range(1, groups):
        inputs[g] = swap(x_own, 2 * g), swap(c_own, 2 * g)
    x_all, c_all, xt_all = gather([inputs[g] for g in range(groups)])
    inputs["all"] = x_all, c_all

    fulls = {}
    received = [None, None]
    outs = [None] * groups
    grads = ()
    marks = []

    def settle(g, h, full):
        fulls[g, h] = full
        lo, hi = h * PIECES * width, (h + 1) * PIECES * width
        wg = lax.slice_in_dim(w_gate, lo, hi, axis=1)
        wu = lax.slice_in_dim(w_up, lo, hi, axis=1)
        wd = lax.slice_in_dim(w_down, lo, hi, axis=0)
        step = (mm(full[0], wd, 1, 0), mm(full[1], wg, 1, 1) + mm(full[2], wu, 1, 1))
        outs[g] = step if outs[g] is None else (outs[g][0] + step[0], outs[g][1] + step[1])
        marks.extend(outs[g])
        if g > 0 and h == WIDE - 1:
            for i in range(2):
                came = swap(outs[g][i].astype(wire), 2 * g).astype(F32)
                received[i] = came if received[i] is None else received[i] + came

    def weigh(h, behind):
        nonlocal grads
        *grads, mark = weight_grads(
            xt_all, c_all, [fulls[g, h] for g in range(groups)], h, hid, grads, behind
        )
        marks.append(mark)

    if mid == 2:
        pairs = [(d, d ^ 1) for d in range(side)]
        steps = len(order)
        step_of = {key: t for t, key in enumerate(order)}
        made = {}
        for c in range(PIECES, last, PIECES):
            made.setdefault(step_of[0, c] - 3, []).append(([0], range(c, c + PIECES)))
        for c in range(0, last, PIECES):
            made.setdefault(step_of[1, c] - 3 + (c == 0), []).append(([1], range(c, c + PIECES)))
        for c in range(last, total_chunks, PIECES):
            made.setdefault(step_of[1, c] - 3, []).append(([0, 1], range(c, c + PIECES)))
        arrived, results = {}, {}

        def depart(t, *behind):
            if t < LAG:
                load = rows_of(sends[order[t]])
            else:
                at_end, start = sends[order[min(t, steps - 1)]]
                load = choose(flags, [at_end], start, [results[t - LAG]], behind)
            arrived[t] = along(load, pairs)
            return load

        depart(0)
        last_made = sends[0, 0][0]
        if PIECES > 1:
            last_made = prepare([0], [1], last_made)
        for t in (-2, -1):
            for gs, chunks in made.get(t, ()):
                last_made = prepare(gs, list(chunks), last_made)
            if t == -2:
                depart(1)
        behind = [last_made]
        w_gate, w_up, w_down = weights = stage(
            [(w, w.shape) for w in (w_gate, w_up, w_down)], behind
        )
        behind = [w_gate]
        waiting = None
        ready = []
        for t in range(steps + LAG):
            started = None
            if t < steps:
                send, keep = combine(arrived[t], *sums[order[t]], 2 * rows, behind)
                started = keep, middle(send)
                behind = [send]
            if waiting is not None:
                results[t - 1] = finish(*waiting, behind)
                behind = [results[t - 1]]
            waiting = started
            later = []
            for gs, chunks in made.get(t, ()):
                if t + 2 in [step_of[g, c] for g in gs for c in chunks]:
                    behind = [prepare(gs, list(chunks), *behind)]
                else:
                    later.append((gs, list(chunks)))
            if t + 2 < steps + LAG:
                load = depart(t + 2, *behind)
                if t + 2 >= LAG:
                    behind = [load]
            for gs, chunks in later:
                behind = [prepare(gs, chunks, *behind)]
            if t >= LAG:
                g, c = order[t - LAG]
                if c % PIECES == PIECES - 1:
                    past = range(t - LAG - PIECES + 1, t - LAG + 1)
                    done = [results[u] for u in past]
                    came = [arrived[u + LAG] for u in past]
                    marks.clear()
                    settle(g, c // PIECES, choose(flags, came, 0, done, behind))
                    behind = list(marks)
            for h in range(WIDE - 1):
                if h not in ready and all((i, h) in fulls for i in range(groups)):
                    ready.append(h)
                    marks.clear()
                    weigh(h, behind)
                    behind = list(marks)
        weigh(WIDE - 1, [])
    else:
        for g in range(groups):
            for h in range(WIDE):
                chunks = [h * PIECES + j for j in range(PIECES)]
                chunks = [c for c in chunks if (g, c) not in sums]
                if chunks:
                    prepare([g], chunks)
                pieces = []
                for c in range(h * PIECES, (h + 1) * PIECES):
                    total = rows_of(sums[g, c])
                    for r in range(mid - 1):
                        moves = [(r, r + 1), (side - 1 - r, side - 2 - r)]
                        total = total + along(total.astype(wire), moves).astype(F32)
                    total = total + middle(total.astype(wire)).astype(F32)
                    full = jnp.stack(results_of(*total))
                    for r in reversed(range(mid - 1)):
                        came = along(full, [(r + 1, r), (side - 2 - r, side - 1 - r)])
                        full = jnp.where((down == r) | (down == side - 1 - r), came, full)
                    pieces.append(full)
                settle(g, h, jnp.concatenate(pieces, 2))
        for h in range(WIDE):
            weigh(h, [])

    halves = [split(flags, received[i] + outs[0][i]) for i in range(2)]
    cames = [swap(send, 1) for send, _ in halves]
    ends = close([keep for _, keep in halves], cames)
    return tuple(end[None] for end in ends) + tuple(g[None] for g in grads)


def solution(mesh):
    spec = P(("groups", "row"), None, None)
    weight = P("row", None, None)
    return jax.shard_map(
        body,
        mesh=mesh,
        in_specs=(spec, weight, weight, weight, spec),
        out_specs=(spec,) * 5,
        check_vma=False,
    )
```

```python
import math

import jax
import jax.numpy as jnp
from jax import lax
from jax.experimental import pallas as pl
from jax.experimental.pallas import tpu as pltpu
from jax.sharding import PartitionSpec as P

BF = jnp.bfloat16
F32 = jnp.float32
WIDE = 4
PIECES = 1
LAG = 3
LATE = 2
MIB = 2**20


def mm(left, right, ldim, rdim):
    return lax.dot_general(
        left, right, (((ldim,), (rdim,)), ((), ())), preferred_element_type=F32
    )


def params(mib):
    return pltpu.CompilerParams(vmem_limit_bytes=mib * MIB)


def partials(x, c, weights, chunks, width, wire, behind):
    m, feat = x.shape
    n = len(chunks)
    k = 5 + len(behind)

    def kernel(*refs):
        x_ref, c_ref, wg_ref, wu_ref, wd_ref = refs[:5]
        for j in range(n):

            @pl.when(pl.program_id(0) == j)
            def _():
                for i, part in enumerate(
                    (
                        mm(x_ref[...], wg_ref[...], 1, 0),
                        mm(x_ref[...], wu_ref[...], 1, 0),
                        mm(c_ref[...], wd_ref[...], 1, 1),
                    )
                ):
                    refs[k + j][i] = part
                    refs[k + n + j][i] = part.astype(wire)

    cols = pl.BlockSpec((feat, width), lambda j: (0, chunks[0] + j))
    whole = pl.BlockSpec((m, feat), lambda j: (0, 0))
    shape = (3, m, width)
    return pl.pallas_call(
        kernel,
        grid=(n,),
        in_specs=[whole, whole, cols, cols, pl.BlockSpec((width, feat), lambda j: (chunks[0] + j, 0))]
        + [REST] * len(behind),
        out_specs=[pl.BlockSpec(shape, lambda j: (0, 0, 0))] * (2 * n),
        out_shape=[in_vmem(shape, F32)] * n + [in_vmem(shape, wire)] * n,
        compiler_params=params(16),
        cost_estimate=pl.CostEstimate(
            flops=6 * m * feat * width * n,
            bytes_accessed=6 * feat * width * n,
            transcendentals=0,
        ),
        name="partials",
    )(x, c, *weights, *behind)


def grads_kernel(n, xt_ref, c_ref, *refs):
    fulls = refs[:n]
    gate_ref, up_ref, down_ref, mark_ref = refs[-4:]
    mark_ref[...] = jnp.zeros_like(mark_ref)
    hidden, gate_delta, up_delta = [
        jnp.concatenate([f[i] for f in fulls], 0) for i in range(3)
    ]
    gate_ref[...] = mm(xt_ref[...], gate_delta, 1, 0)
    up_ref[...] = mm(xt_ref[...], up_delta, 1, 0)
    down_ref[...] = mm(hidden, c_ref[...], 0, 0)


def weight_grads(xt, c, fulls, h, hid, before, behind):
    feat, tok = xt.shape
    slab = fulls[0].shape[2]
    rows = fulls[0].shape[1]
    bn = min(256, slab)
    nb = slab // bn
    n = len(fulls)
    cols = pl.BlockSpec((feat, bn), lambda j: (0, h * nb + j))
    return pl.pallas_call(
        lambda *refs: grads_kernel(n, *refs),
        grid=(nb,),
        in_specs=[
            pl.BlockSpec((feat, tok), lambda j: (0, 0)),
            pl.BlockSpec((tok, feat), lambda j: (0, 0)),
        ]
        + [pl.BlockSpec((3, rows, bn), lambda j: (0, 0, j))] * n
        + [REST] * (len(before) + len(behind)),
        out_specs=[
            cols,
            cols,
            pl.BlockSpec((bn, feat), lambda j: (h * nb + j, 0)),
            pl.BlockSpec((8, 128), lambda j: (0, 0)),
        ],
        out_shape=[
            jax.ShapeDtypeStruct((feat, hid), F32),
            jax.ShapeDtypeStruct((feat, hid), F32),
            jax.ShapeDtypeStruct((hid, feat), F32),
            jax.ShapeDtypeStruct((8, 128), F32),
        ],
        input_output_aliases={2 + n + i: i for i in range(len(before))},
        compiler_params=params(16),
        cost_estimate=pl.CostEstimate(
            flops=6 * tok * feat * slab,
            bytes_accessed=12 * feat * slab,
            transcendentals=0,
        ),
        name="weight_grads",
    )(xt, c, *fulls, *before, *behind)


def in_hbm(values):
    return pltpu.with_memory_space_constraint(values, pltpu.HBM)


def in_vmem(shape, dtype):
    return pltpu.VMEM(shape, dtype)


HERE = pl.BlockSpec(memory_space=pltpu.VMEM)
FLAG = pl.BlockSpec(memory_space=pltpu.SMEM)
REST = pl.BlockSpec(memory_space=pl.ANY)


def results_of(gate, up, hidden_grad):
    sigma = jax.nn.sigmoid(gate)
    activated = gate * sigma
    return (
        (activated * up).astype(BF),
        (hidden_grad * up * sigma * (1.0 + gate * (1.0 - sigma))).astype(BF),
        (hidden_grad * activated).astype(BF),
    )


def small(kernel, name, shapes, args, flags=(), behind=(), mib=4, spec=HERE):
    n = len(flags) + len(args)
    m = n + len(behind)
    size = sum(math.prod(a.shape) * 2 for a in list(args) + list(shapes))
    return pl.pallas_call(
        lambda *refs: kernel(*refs[:n], *refs[m:]),
        in_specs=[FLAG] * len(flags) + [spec] * len(args) + [REST] * len(behind),
        out_specs=[HERE] * len(shapes),
        out_shape=list(shapes),
        compiler_params=params(mib),
        cost_estimate=pl.CostEstimate(flops=size, bytes_accessed=size, transcendentals=0),
        name=name,
    )(*flags, *args, *behind)


def combine(came, part, start, rows, behind):
    def kernel(came_ref, part_ref, send_ref, keep_ref):
        total = came_ref[...].astype(F32) + part_ref[:, start : start + rows]
        keep_ref[...] = total
        send_ref[...] = total.astype(BF)

    shape = came.shape
    return small(
        kernel, "combine", [in_vmem(shape, BF), in_vmem(shape, F32)], [came, part], (), behind
    )


def finish(keep, came, behind):
    def kernel(keep_ref, came_ref, done_ref):
        own = [keep_ref[i] + came_ref[i].astype(F32) for i in range(3)]
        for i, values in enumerate(results_of(*own)):
            done_ref[i] = values

    return small(
        kernel, "finish", [in_vmem(keep.shape, BF)], [keep, came], (), behind
    )[0]


def stage(pieces, behind=()):
    n = len(pieces)
    m = n + len(behind)
    shapes = [shape for _, shape in pieces]
    cuts = [max(1, shape[0] // 256) for shape in shapes]

    def kernel(*refs):
        sems = refs[-1]
        copies = []
        for i, shape in enumerate(shapes):
            size = shape[0] // cuts[i]
            for j in range(cuts[i]):
                part = pl.ds(j * size, size)
                copies.append(
                    pltpu.make_async_copy(
                        refs[i].at[part, pl.ds(0, shape[1])],
                        refs[m + i].at[part],
                        sems.at[len(copies)],
                    )
                )
        for copy in copies:
            copy.start()
        for copy in copies:
            copy.wait()

    size = sum(math.prod(shape) * 2 for shape in shapes)
    return pl.pallas_call(
        kernel,
        in_specs=[REST] * m,
        out_specs=[HERE] * n,
        out_shape=[in_vmem(shape, BF) for shape in shapes],
        scratch_shapes=[pltpu.SemaphoreType.DMA((sum(cuts),))],
        compiler_params=params(4),
        cost_estimate=pl.CostEstimate(flops=size, bytes_accessed=size, transcendentals=0),
        name="stage",
    )(*[in_hbm(values) for values, _ in pieces], *behind)


def close(keep, came):
    n, rows, feat = keep.shape

    def kernel(keep_ref, came_ref, *refs):
        for i in range(n):
            refs[i][...] = (keep_ref[i] + came_ref[i]).astype(BF)

    return pl.pallas_call(
        kernel,
        in_specs=[HERE] * 2,
        out_shape=[jax.ShapeDtypeStruct((rows, feat), BF)] * n,
        compiler_params=params(4),
        name="close",
    )(keep, came)


def gather(pairs):
    n = len(pairs)
    rows, feat = pairs[0][0].shape

    def kernel(*refs):
        x_ref, c_ref, xt_ref = refs[2 * n :]
        for i in range(n):
            cut = slice(i * rows, (i + 1) * rows)
            x_ref[cut] = refs[i][...]
            c_ref[cut] = refs[n + i][...]
            xt_ref[:, cut] = refs[i][...].T

    tok = n * rows
    return small(
        kernel,
        "gather",
        [in_vmem((tok, feat), BF), in_vmem((tok, feat), BF), in_vmem((feat, tok), BF)],
        [p[0] for p in pairs] + [p[1] for p in pairs],
        mib=8,
    )


def pair(flags, blocks):
    rows, feat = blocks[0].shape

    def kernel(flag_ref, *refs):
        for a_ref, b_ref, out_ref in (refs[0:2] + refs[4:5], refs[2:4] + refs[5:6]):

            @pl.when(flag_ref[0] % 2 == 0)
            def _():
                out_ref[:rows] = a_ref[...]
                out_ref[rows:] = b_ref[...]

            @pl.when(flag_ref[0] % 2 == 1)
            def _():
                out_ref[:rows] = b_ref[...]
                out_ref[rows:] = a_ref[...]

    return small(kernel, "pair", [in_vmem((2 * rows, feat), BF)] * 2, blocks, [flags])


def split(flags, values):
    n = len(values)
    rows, feat = values[0].shape[0] // 2, values[0].shape[1]

    def kernel(flag_ref, *refs):
        send_ref, keep_ref = refs[n:]
        for flag in range(2):

            @pl.when(flag_ref[0] % 2 == flag)
            def _():
                for i in range(n):
                    keep_ref[i] = refs[i][flag * rows : (flag + 1) * rows]
                    send_ref[i] = refs[i][(1 - flag) * rows : (2 - flag) * rows]

    return small(kernel, "split", [in_vmem((n, rows, feat), F32)] * 2, values, [flags])


def choose(flags, at_end, start, done, behind):
    rows, width = done[0].shape[1:]
    n = len(at_end)

    def kernel(flag_ref, *refs):
        for j in range(n):
            cols = slice(j * width, (j + 1) * width)

            @pl.when(flag_ref[0] >= 2)
            def _():
                refs[-1][:, :, cols] = refs[j][:, start : start + rows]

            @pl.when(flag_ref[0] < 2)
            def _():
                refs[-1][:, :, cols] = refs[n + j][...]

    shape = in_vmem((3, rows, n * width), BF)
    return small(kernel, "choose", [shape], [*at_end, *done], [flags], behind)[0]


def body(tokens, gate_weight, up_weight, down_weight, cotangent):
    count = lax.axis_size("row")
    side = math.isqrt(count)
    place = lax.axis_index("row")
    across = place % side
    down = place // side
    core = across % 2
    groups = side // 2
    mid = side // 2
    wire = BF if side <= 4 else F32

    w_gate = gate_weight[0]
    w_up = up_weight[0]
    w_down = down_weight[0]
    hid = w_gate.shape[1]
    rows = tokens.shape[1]
    total_chunks = WIDE * PIECES
    width = hid // total_chunks

    def swap(values, bits):
        return lax.ppermute(values, "row", [(i, i ^ bits) for i in range(count)])

    def along(values, moves):
        route = [
            (src * side + i, dst * side + i) for src, dst in moves for i in range(side)
        ]
        return lax.ppermute(values, "row", route)

    def middle(values):
        route = []
        for d in range(side):
            for i in range(side):
                to = (side - 1 - d, i) if d in (mid - 1, mid) else (d, i ^ 1)
                route.append((d * side + i, to[0] * side + to[1]))
        return lax.ppermute(values, "row", route)

    is_end = ((down == 0) | (down == side - 1)).astype(jnp.int32)
    flags = (core + 2 * is_end).reshape(1)

    slab = width * PIECES
    feat = w_gate.shape[0]
    early = [(w_gate, (feat, slab)), (w_up, (feat, slab)), (w_down, (slab, feat))]
    x_mine, c_mine, *weights = stage(
        [(tokens[0], tokens.shape[1:]), (cotangent[0], tokens.shape[1:])] + early
    )
    x_own, c_own = pair(
        flags,
        [x_mine, swap(tokens[0], 1), c_mine, swap(cotangent[0], 1)],
    )
    last = total_chunks - PIECES * LATE
    order = [(0, c) for c in range(last)]
    order += [(g, c) for g in range(1, groups) for c in range(total_chunks)]
    order += [(0, c) for c in range(last, total_chunks)]
    sums, sends = {}, {}
    inputs = {0: (x_own, c_own)}

    def prepare(gs, chunks, *behind):
        x, c = inputs[gs[0]] if len(gs) == 1 else inputs["all"]
        made = partials(x, c, weights, chunks, width, wire, behind)
        for j, chunk in enumerate(chunks):
            for n, g in enumerate(gs):
                sums[g, chunk] = made[j], 2 * rows * n
                sends[g, chunk] = made[len(chunks) + j], 2 * rows * n
        return made[0]

    def rows_of(entry):
        values, start = entry
        return lax.slice_in_dim(values, start, start + 2 * rows, axis=1)

    prepare([0], [0])
    weights = [in_hbm(w) for w in (w_gate, w_up, w_down)]
    for g in range(1, groups):
        inputs[g] = swap(x_own, 2 * g), swap(c_own, 2 * g)
    x_all, c_all, xt_all = gather([inputs[g] for g in range(groups)])
    inputs["all"] = x_all, c_all

    fulls = {}
    received = [None, None]
    outs = [None] * groups
    grads = ()
    marks = []

    def settle(g, h, full):
        fulls[g, h] = full
        lo, hi = h * PIECES * width, (h + 1) * PIECES * width
        wg = lax.slice_in_dim(w_gate, lo, hi, axis=1)
        wu = lax.slice_in_dim(w_up, lo, hi, axis=1)
        wd = lax.slice_in_dim(w_down, lo, hi, axis=0)
        step = (mm(full[0], wd, 1, 0), mm(full[1], wg, 1, 1) + mm(full[2], wu, 1, 1))
        outs[g] = step if outs[g] is None else (outs[g][0] + step[0], outs[g][1] + step[1])
        marks.extend(outs[g])
        if g > 0 and h == WIDE - 1:
            for i in range(2):
                came = swap(outs[g][i].astype(wire), 2 * g).astype(F32)
                received[i] = came if received[i] is None else received[i] + came

    def weigh(h, behind):
        nonlocal grads
        *grads, mark = weight_grads(
            xt_all, c_all, [fulls[g, h] for g in range(groups)], h, hid, grads, behind
        )
        marks.append(mark)

    if mid == 2:
        pairs = [(d, d ^ 1) for d in range(side)]
        steps = len(order)
        step_of = {key: t for t, key in enumerate(order)}
        made = {}
        for c in range(PIECES, last, PIECES):
            made.setdefault(step_of[0, c] - 3, []).append(([0], range(c, c + PIECES)))
        for c in range(0, last, PIECES):
            made.setdefault(step_of[1, c] - 3 + (c == 0), []).append(([1], range(c, c + PIECES)))
        for c in range(last, total_chunks, PIECES):
            made.setdefault(step_of[1, c] - 3, []).append(([0, 1], range(c, c + PIECES)))
        arrived, results = {}, {}

        def depart(t, *behind):
            if t < LAG:
                load = rows_of(sends[order[t]])
            else:
                at_end, start = sends[order[min(t, steps - 1)]]
                load = choose(flags, [at_end], start, [results[t - LAG]], behind)
            arrived[t] = along(load, pairs)
            return load

        depart(0)
        last_made = sends[0, 0][0]
        if PIECES > 1:
            last_made = prepare([0], [1], last_made)
        for t in (-2, -1):
            for gs, chunks in made.get(t, ()):
                last_made = prepare(gs, list(chunks), last_made)
            if t == -2:
                depart(1)
        behind = [last_made]
        w_gate, w_up, w_down = weights = stage(
            [(w, w.shape) for w in (w_gate, w_up, w_down)], behind
        )
        behind = [w_gate]
        waiting = None
        ready = []
        for t in range(steps + LAG):
            started = None
            if t < steps:
                send, keep = combine(arrived[t], *sums[order[t]], 2 * rows, behind)
                started = keep, middle(send)
                behind = [send]
            if waiting is not None:
                results[t - 1] = finish(*waiting, behind)
                behind = [results[t - 1]]
            waiting = started
            later = []
            for gs, chunks in made.get(t, ()):
                if t + 2 in [step_of[g, c] for g in gs for c in chunks]:
                    behind = [prepare(gs, list(chunks), *behind)]
                else:
                    later.append((gs, list(chunks)))
            if t + 2 < steps + LAG:
                load = depart(t + 2, *behind)
                if t + 2 >= LAG:
                    behind = [load]
            for gs, chunks in later:
                behind = [prepare(gs, chunks, *behind)]
            if t >= LAG:
                g, c = order[t - LAG]
                if c % PIECES == PIECES - 1:
                    past = range(t - LAG - PIECES + 1, t - LAG + 1)
                    done = [results[u] for u in past]
                    came = [arrived[u + LAG] for u in past]
                    marks.clear()
                    settle(g, c // PIECES, choose(flags, came, 0, done, behind))
                    behind = list(marks)
            for h in range(WIDE - 1):
                if h not in ready and all((i, h) in fulls for i in range(groups)):
                    ready.append(h)
                    marks.clear()
                    weigh(h, behind)
                    behind = list(marks)
        weigh(WIDE - 1, [])
    else:
        for g in range(groups):
            for h in range(WIDE):
                chunks = [h * PIECES + j for j in range(PIECES)]
                chunks = [c for c in chunks if (g, c) not in sums]
                if chunks:
                    prepare([g], chunks)
                pieces = []
                for c in range(h * PIECES, (h + 1) * PIECES):
                    total = rows_of(sums[g, c])
                    for r in range(mid - 1):
                        moves = [(r, r + 1), (side - 1 - r, side - 2 - r)]
                        total = total + along(total.astype(wire), moves).astype(F32)
                    total = total + middle(total.astype(wire)).astype(F32)
                    full = jnp.stack(results_of(*total))
                    for r in reversed(range(mid - 1)):
                        came = along(full, [(r + 1, r), (side - 2 - r, side - 1 - r)])
                        full = jnp.where((down == r) | (down == side - 1 - r), came, full)
                    pieces.append(full)
                settle(g, h, jnp.concatenate(pieces, 2))
        for h in range(WIDE):
            weigh(h, [])

    send, keep = split(flags, [received[i] + outs[0][i] for i in range(2)])
    ends = close(keep, swap(send, 1))
    return tuple(end[None] for end in ends) + tuple(g[None] for g in grads)


def solution(mesh):
    spec = P(("groups", "row"), None, None)
    weight = P("row", None, None)
    return jax.shard_map(
        body,
        mesh=mesh,
        in_specs=(spec, weight, weight, weight, spec),
        out_specs=(spec,) * 5,
        check_vma=False,
    )
```
